32 devices in a mesh: period: 16 (over z, y, x), half: 2 (over core).
Axes of the slice: x: 2, y: 2, z: 4, core: 2. Of those that a mesh axis runs over, the one named last changes fastest.
Arguments:
- probes: float32 [128, 4, 512], P('period', None, 'half'), may hold values from -6 to 6
- footprints: bfloat16 [128, 512, 512], P('period', None, 'half'), may hold values from -0.25 to 0.25
- lag_weights: float32 [128, 4], P('period'), may hold values from 0.2 to 2
- owners: int32 [128, 4], P('period'), may hold values from 0 to 15, all different within a row; in each aligned block of 8 rows (0 to 7, 8 to 15, ...) at most 4 rows name the same one
- window_tiles: int32 [128, 2], P('period', 'half'), may hold values from 0 to 10
- coords: int32 [2, 3072], replicated, may hold values from 0 to 63
- temporal: float32 [16, 16], replicated, as said below
Outputs:
- coefficients: float32 [4, 4], replicated
- residual: float32 [128, 4, 512], P('period', None, 'half')
The draws below stay inside these ranges and needn't reach their ends.
Inputs may be any that keep to these rules, and one draw needn't show every extreme that they name: `owners`: each row names 4 different periods. Among the 8 rows of one index of period, no period is named more than 4 times, and one is named exactly 4 times. `temporal`: symmetric.
All inputs are finite; a program needn't handle non-finite values.
Results may differ from the reference program's by a relative error of at most 0.025.
Values may be sent and summed in bfloat16 or wider, within the bound.
A program may use at most 64 MiB of HBM per device.

```python
import math
import jax
import jax.numpy as jnp
import numpy as np
from jax import lax

CELLS = 3072
WIN = 256
SOUND = 512
TOP = 4
GRID = 64
PROBES = 4
BLK_DEV = 8
PERIODS = 16
BLOCKS = 128
CAP = 4
N_PERIOD = 16


def draw_temporal(key, part):
    key_sym, key_diag = jax.random.split(jax.random.fold_in(key, 17))
    raw = jax.random.normal(key_sym, (PERIODS, PERIODS), jnp.float32)
    symmetric = (raw + raw.T) * (0.6 / jnp.sqrt(2.0 * PERIODS))
    diagonal = jax.random.uniform(key_diag, (PERIODS,), jnp.float32, minval=0.5, maxval=1.5)
    return symmetric + jnp.diag(diagonal)


def set_ends(result, rng, low, top_value):
    extent = result.shape
    place = [jax.random.randint(jax.random.fold_in(rng, axis), (), 0, extent[axis]) for axis in range(len(extent))]
    result = result.at[tuple(place)].set(low)
    longest = extent.index(max(extent))
    place[longest] = (place[longest] + 1) % extent[longest]
    return result.at[tuple(place)].set(top_value)


def level_of(key, dims, cuts, least, high):
    loudness, own = 1.0, jax.random.fold_in(key, 6)
    for position, shards_of in cuts:
        heights = jnp.exp(jax.random.uniform(jax.random.fold_in(own, position), (shards_of,), jnp.float32, least / len(cuts), high / len(cuts)))
        loudness = loudness * jnp.repeat(heights, dims[position] // shards_of).reshape([-1 if axis == position else 1 for axis in range(len(dims))])
    return loudness


def assign_block(rng, own, number, rows, amount, top, bound, skew):
    ranking = jax.random.permutation(rng, amount)
    crowded, common = load_shares(amount, rows * top, bound, skew, True), load_shares(amount, rows * top, bound, skew, False)
    places = jnp.arange(amount)

    def named(lengths, rotation):
        used = int((lengths > 0).sum())
        fixed = max(1, used // 4)
        shifted = fixed + (places - fixed + rotation * (used - fixed)) % max(1, amount - fixed)
        return jnp.zeros((amount,), jnp.int32).at[ranking[jnp.where(places < fixed, places, shifted)]].set(jnp.asarray(lengths, jnp.int32))

    lengths = jnp.where(number % 4 == 0, named(crowded, number // 4), named(common, number - number // 4 - 1))
    mixed = jax.random.permutation(jax.random.fold_in(own, 3), amount)
    source_of, receiver = mixed[0:amount // 2 * 2:2], mixed[1:amount // 2 * 2:2]
    slack = jnp.minimum(lengths[source_of] - 1, bound - lengths[receiver]) // 2
    slack = jnp.where((source_of == ranking[0]) | (receiver == ranking[0]) | (lengths[receiver] == 0), 0, jnp.maximum(slack, 0))
    shifted = jax.random.randint(jax.random.fold_in(own, 4), (amount // 2,), 0, 1 << 20) % (slack + 1)
    lengths = lengths.at[source_of].add(-shifted).at[receiver].add(shifted)
    items = jnp.searchsorted(jnp.cumsum(lengths), jnp.arange(rows * top), side="right").astype(jnp.int32)
    grid = items.reshape(top, rows).T
    grid = grid[jax.random.permutation(jax.random.fold_in(own, 1), rows)]
    rotation = jax.random.randint(jax.random.fold_in(own, 2), (rows, 1), 0, top)
    return jnp.take_along_axis(grid, (jnp.arange(top)[None, :] + rotation) % top, axis=1)


def load_shares(number_of, total, limit, slope, full):
    portions = [(1 << 20) // math.isqrt(standing ** slope) + 1 for standing in range(1, number_of + 1)]
    largest = limit if full else min(limit, max(-(-total // number_of), total * portions[0] // sum(portions)))
    least = 1 if total - largest >= number_of - 1 else 0
    given, rest = [largest] + [least] * (number_of - 1), total - largest - least * (number_of - 1)
    while rest > 0:
        candidates = [i for i in range(1, number_of) if given[i] < largest] or [i for i in range(1, number_of) if given[i] < limit]
        mass, left = sum([portions[i] for i in candidates]), rest
        for i in candidates:
            addition = min(limit - given[i], max(1, left * portions[i] // mass), rest)
            given[i] = given[i] + addition
            rest = rest - addition
    return np.array(given)


def noise(key, dims, width, reach, cuts=(), held_as=jnp.bfloat16):
    values = jax.random.normal(key, dims, jnp.float32) * width
    if len(cuts) > 0:
        values = level_of(key, dims, cuts, -0.22, 0.18) * values
    return jnp.clip(values, min=-reach, max=reach).astype(held_as)


def setup_inputs(seed: int = 0) -> dict:
    keys = jax.random.split(jax.random.key(seed), 8)
    probes = noise(keys[0], (BLOCKS, PROBES, SOUND), 1.0, 6.0, ((0, 16), (2, 2)), jnp.float32)
    footprints = noise(keys[1], (BLOCKS, SOUND, 2 * WIN), (2 * WIN) ** -0.5, 0.25, ((0, 16), (2, 2)))
    lag_weights = jnp.clip(jnp.exp(math.log(2.0) - 2.3025851 * jax.random.uniform(keys[2], (BLOCKS, TOP), jnp.float32) ** level_of(keys[2], (BLOCKS, TOP), ((0, 16),), -0.2, 0.2)), 0.2, 2.0)
    owners_keys = jax.random.split(jax.random.fold_in(keys[3], 1), BLOCKS // BLK_DEV)
    owners_turns = jax.random.permutation(jax.random.fold_in(keys[3], 3), BLOCKS // BLK_DEV)
    owners = jax.vmap(lambda own, number: assign_block(jax.random.fold_in(keys[3], 2), own, number, BLK_DEV, N_PERIOD, TOP, CAP, 2))(owners_keys, owners_turns).reshape((BLOCKS, TOP))
    window_tiles = set_ends(jax.random.randint(keys[4], (BLOCKS, 2), 0, CELLS // 256 - WIN // 128 + 1), jax.random.fold_in(keys[4], 1), 0, (CELLS // 256 - WIN // 128 + 1) - 1).astype(jnp.int32)
    coords = set_ends(jax.random.randint(keys[5], (2, CELLS), 0, GRID), jax.random.fold_in(keys[5], 1), 0, GRID - 1).astype(jnp.int32)
    temporal = draw_temporal(jax.random.fold_in(keys[7], 71), 0)
    return dict(probes=probes, footprints=footprints, lag_weights=lag_weights, owners=owners, window_tiles=window_tiles, coords=coords, temporal=temporal)


epsilon = 1e-06
kernel_scale = 0.05
kernel_length = 6.0
highest = lax.Precision.HIGHEST

def spatial_kernel(coords):
    delta_x = coords[0][:, None] - coords[0][None, :]
    delta_y = coords[1][:, None] - coords[1][None, :]
    squared = (delta_x * delta_x + delta_y * delta_y).astype(jnp.float32)
    return kernel_scale * jnp.exp(-jnp.sqrt(squared) / kernel_length)

def window_cells(window_tiles):
    half_cells = CELLS // 2
    offsets = jnp.arange(WIN, dtype=jnp.int32)
    first_half = window_tiles[:, 0:1] * 128 + offsets[None, :]
    second_half = half_cells + window_tiles[:, 1:2] * 128 + offsets[None, :]
    return jnp.concatenate([first_half, second_half], axis=1).astype(jnp.int32)

def apply_operator(vector, footprints, lag_weights, owners, cells, kernel, temporal):
    vector_low = vector.astype(jnp.bfloat16).reshape(N_PERIOD, BLK_DEV, PROBES, SOUND)
    foot_blocks = footprints.reshape(N_PERIOD, BLK_DEV, SOUND, 2 * WIN)
    weight_blocks = lag_weights.reshape(N_PERIOD, BLK_DEV, TOP)
    owner_blocks = owners.reshape(N_PERIOD, BLK_DEV, TOP)
    cell_blocks = cells.reshape(N_PERIOD, BLK_DEV, 2 * WIN)
    probe_index = jnp.arange(PROBES, dtype=jnp.int32)[None, None, :, None]

    def adjoint_group(flux, members):
        low_group, foot_group, weight_group, owner_group, cell_group = members
        partial_value = jnp.einsum('bps,bsw->bpw', low_group.astype(jnp.float32), foot_group.astype(jnp.float32))
        terms = weight_group[:, :, None, None] * partial_value[:, None, :, :]
        flux = flux.at[owner_group[:, :, None, None], probe_index, cell_group[:, None, None, :]].add(terms)
        return (flux, None)
    flux_start = jnp.zeros((N_PERIOD, PROBES, CELLS), jnp.float32)
    flux, unused = lax.scan(adjoint_group, flux_start, (vector_low, foot_blocks, weight_blocks, owner_blocks, cell_blocks))
    spatial = jnp.einsum('npc,rc->npr', flux, kernel, precision=highest)
    field = jnp.einsum('tn,npr->tpr', temporal, spatial, precision=highest).astype(jnp.bfloat16)

    def forward_group(carry, members):
        foot_group, weight_group, owner_group, cell_group = members
        windows = field[owner_group[:, :, None, None], probe_index, cell_group[:, None, None, :]]
        sounded = jnp.einsum('bk,bkpw,bsw->bps', weight_group, windows.astype(jnp.float32), foot_group.astype(jnp.float32))
        return (carry, sounded)
    carry, images = lax.scan(forward_group, jnp.zeros((), jnp.float32), (foot_blocks, weight_blocks, owner_blocks, cell_blocks))
    return images.reshape(BLOCKS, PROBES, SOUND)

def reference(probes, footprints, lag_weights, owners, window_tiles, coords, temporal):
    kernel = spatial_kernel(coords)
    cells = window_cells(window_tiles)
    total_rows = float(BLOCKS * SOUND)

    def mean_of(values):
        return lax.optimization_barrier(jnp.sum(values, axis=(0, 2))) / total_rows
    start_scale = jnp.sqrt(mean_of(probes * probes) + epsilon)
    first_q = probes / start_scale[None, :, None]
    image_one = apply_operator(first_q, footprints, lag_weights, owners, cells, kernel, temporal)
    alpha_one = mean_of(first_q * image_one)
    rest_one = image_one - alpha_one[None, :, None] * first_q
    beta_one = jnp.sqrt(mean_of(rest_one * rest_one) + epsilon)
    second_q = rest_one / beta_one[None, :, None]
    image_two = apply_operator(second_q, footprints, lag_weights, owners, cells, kernel, temporal)
    image_two = image_two - beta_one[None, :, None] * first_q
    alpha_two = mean_of(second_q * image_two)
    residual = image_two - alpha_two[None, :, None] * second_q
    beta_two = jnp.sqrt(mean_of(residual * residual) + epsilon)
    coefficients = jnp.stack([alpha_one, beta_one, alpha_two, beta_two], axis=0)
    return (coefficients, residual)
```

```python
import functools
import math

import jax
import jax.numpy as jnp
from jax import lax
from jax.experimental import pallas as pl
from jax.experimental.pallas import tpu as pltpu
from jax.sharding import PartitionSpec as P

epsilon = 1e-06
kernel_scale = 0.05
kernel_length = 6.0
highest = lax.Precision.HIGHEST
MESH = pl.DeviceIdType.MESH
F32 = jnp.float32
BF16 = jnp.bfloat16
LANES = 128
early_tiles = 4


def kernel(
    n,
    probes_ref,
    foot_hbm,
    lag_ref,
    owner_ref,
    tile_ref,
    coords_ref,
    temporal_ref,
    coef_ref,
    residual_ref,
    foot,
    pbuf,
    meta,
    terms,
    stats,
    flux_out,
    flux_in,
    image_out,
    image_in,
    kbuf,
    zt,
    foot_sem,
    pair_send,
    pair_recv,
    peer_send,
    peer_recv,
):
    me = lax.axis_index("period")
    half = lax.axis_index("half")
    blocks, probes_n, half_sounds = probes_ref.shape
    sounds, window = foot.shape[1:]
    win_tiles = window // LANES
    half_cells = coords_ref.shape[1] // 2
    tiles = half_cells // LANES
    rows = probes_n * blocks
    total = float(n * blocks * sounds)

    fetch = pltpu.make_async_copy(foot_hbm, foot, foot_sem)
    fetch.start()

    barrier = pltpu.get_barrier_semaphore()

    def greet(k, carry):
        pl.semaphore_signal(
            barrier, inc=1, device_id={"period": lax.rem(me + k, n)}, device_id_type=MESH
        )
        return carry

    lax.fori_loop(1, n, greet, 0)
    pl.semaphore_signal(barrier, inc=1, device_id={"half": 1 - half}, device_id_type=MESH)

    def pair_copy(source, target, which):
        return pltpu.make_async_remote_copy(
            src_ref=source,
            dst_ref=target,
            send_sem=pair_send.at[which],
            recv_sem=pair_recv.at[which],
            device_id={"half": 1 - half},
            device_id_type=MESH,
        )

    def peer_copy(slots, slot, which, k):
        return pltpu.make_async_remote_copy(
            src_ref=slots.at[slot],
            dst_ref=slots.at[slot],
            send_sem=peer_send.at[which, k],
            recv_sem=peer_recv.at[which, k],
            device_id={"period": lax.rem(me + k, n)},
            device_id_type=MESH,
        )

    def share(slots, which):
        def step(k, carry):
            peer_copy(slots, me, which, k).start()
            return carry

        lax.fori_loop(1, n, step, 0)

    def collect(slots, which):
        def step(k, carry):
            peer_copy(slots, lax.rem(me + n - k, n), which, k).wait_recv()
            return carry

        lax.fori_loop(1, n, step, 0)

    def drain(slots, which):
        def step(k, carry):
            peer_copy(slots, me, which, k).wait_send()
            return carry

        lax.fori_loop(1, n, step, 0)

    for p in range(probes_n):
        pbuf[half, p * blocks : (p + 1) * blocks, :] = probes_ref[:, p, :]

    span = meta.shape[2]
    lane = lax.broadcasted_iota(jnp.int32, (blocks, span), 1)
    weight = jnp.zeros((blocks, span), F32)
    for k in range(lag_ref.shape[1]):
        weight = weight + jnp.where(owner_ref[:, k : k + 1] == lane, lag_ref[:, k : k + 1], 0.0)
    tile_wide = jnp.broadcast_to(tile_ref[:, 0:1], (blocks, span))
    meta[me] = jnp.concatenate(
        [
            jnp.where(lane == span - 1, (tile_wide + j).astype(F32), weight)
            for j in range(win_tiles)
        ],
        axis=0,
    )

    pl.semaphore_wait(barrier, n)
    send_probes = pair_copy(pbuf.at[half], pbuf.at[half], 0)
    send_probes.start()
    share(meta, 0)

    length = math.log2(math.e) / kernel_length

    def cells(axis, start, count):
        picked = coords_ref[axis : axis + 1, pl.ds(pl.multiple_of(start, LANES), count)]
        return picked.astype(F32) * length

    out_x = cells(0, half * half_cells, half_cells)
    out_y = cells(1, half * half_cells, half_cells)
    wide = kbuf.shape[2]

    def build(i, carry):
        own = i < tiles
        side = jnp.where(own, half, 1 - half)
        start = side * half_cells + jnp.where(own, i, i - tiles) * LANES
        in_x = jnp.transpose(jnp.broadcast_to(cells(0, start, LANES), (LANES, LANES)))
        in_y = jnp.transpose(jnp.broadcast_to(cells(1, start, LANES), (LANES, LANES)))
        at = pl.multiple_of(i * LANES, LANES)
        for t in range(tiles):
            dx = in_x - out_x[:, t * LANES : (t + 1) * LANES]
            dy = in_y - out_y[:, t * LANES : (t + 1) * LANES]
            squared = dx * dx + dy * dy
            distance = squared * lax.rsqrt(jnp.maximum(squared, 1e-20))
            lo = t * LANES % wide
            kbuf[t * LANES // wide, pl.ds(at, LANES), lo : lo + LANES] = jnp.exp2(
                -distance
            ).astype(BF16)
        return carry

    lax.fori_loop(0, early_tiles, build, 0)

    row_block = lax.rem(lax.broadcasted_iota(jnp.int32, (rows, LANES), 0), blocks)

    def own_rows(values, b):
        keep = jnp.concatenate([row_block] * (values.shape[1] // LANES), axis=1) == b
        return jnp.where(keep, values, 0.0)

    def back(vector, step):
        part = jnp.zeros((rows, window), F32)
        for b in range(blocks):
            part = part + jnp.dot(
                own_rows(vector, b).astype(BF16), foot[b], preferred_element_type=F32
            )
        by_tile = [
            jnp.concatenate(
                [
                    part[p * blocks : (p + 1) * blocks, j * LANES : (j + 1) * LANES]
                    for p in range(probes_n)
                ],
                axis=1,
            )
            for j in range(win_tiles)
        ]
        terms[step, me] = jnp.concatenate(by_tile, axis=0).astype(BF16)
        share(terms.at[step], 1 + step)

    tile_rows = jnp.concatenate(
        [jnp.broadcast_to(tile_ref[:, 0:1], (blocks, LANES))] * probes_n, axis=0
    )

    def forth(mixer, step):
        collect(terms.at[step], 1 + step)
        shared = terms[step].reshape(n * win_tiles * blocks, probes_n * LANES)
        flux = jnp.dot(mixer[0], shared, preferred_element_type=F32) + jnp.dot(
            mixer[1], shared, preferred_element_type=F32
        )
        flux_out[step] = jnp.concatenate(
            [
                jnp.concatenate(
                    [
                        flux[t * blocks : (t + 1) * blocks, p * LANES : (p + 1) * LANES]
                        for t in range(tiles)
                    ],
                    axis=1,
                )
                for p in range(probes_n)
            ],
            axis=0,
        ).astype(BF16)
        swap = pair_copy(flux_out.at[step], flux_in.at[step], 1 + 2 * step)
        swap.start()
        each = wide // LANES

        def own_part(c, carry):
            got = jnp.dot(
                flux_out[step], kbuf[c, 0:half_cells, :], preferred_element_type=F32
            )
            for e in range(each):
                zt[c * each + e] = got[:, e * LANES : (e + 1) * LANES]
            return carry

        def other_part(c, carry):
            got = jnp.dot(
                flux_in[step],
                kbuf[c, half_cells : 2 * half_cells, :],
                preferred_element_type=F32,
            )
            for e in range(each):
                zt[c * each + e] += got[:, e * LANES : (e + 1) * LANES]
            return carry

        lax.fori_loop(0, kbuf.shape[0], own_part, 0)
        swap.wait()
        lax.fori_loop(0, kbuf.shape[0], other_part, 0)
        parts = []
        for j in range(win_tiles):
            picked = jnp.zeros((rows, LANES), F32)
            for t in range(tiles):
                picked = jnp.where(tile_rows + j == t, zt[t], picked)
            parts.append(picked)
        windows = jnp.concatenate(parts, axis=1)
        image = jnp.zeros((rows, sounds), F32)
        for b in range(blocks):
            image = image + lax.dot_general(
                own_rows(windows, b).astype(BF16),
                foot[b],
                (((1,), (1,)), ((), ())),
                preferred_element_type=F32,
            )
        image_out[step] = image
        swap = pair_copy(image_out.at[step], image_in.at[step], 2 + 2 * step)
        swap.start()
        swap.wait()
        return image + image_in[step]

    def folded(left, right):
        products = left * right
        wide_sum = products[:, 0:LANES]
        for e in range(1, sounds // LANES):
            wide_sum = wide_sum + products[:, e * LANES : (e + 1) * LANES]
        return [
            jnp.sum(wide_sum[p * blocks : (p + 1) * blocks], axis=0, keepdims=True)
            for p in range(probes_n)
        ]

    def start_sums(pairs, step):
        found = []
        for left, right in pairs:
            found += folded(left, right)
        found.append(jnp.zeros((stats.shape[2] - len(found), LANES), F32))
        stats[step, me] = jnp.concatenate(found, axis=0)
        share(stats.at[step], 3 + step)

    def end_sums(step):
        collect(stats.at[step], 3 + step)
        summed = jnp.sum(jnp.sum(stats[step], axis=0), axis=1, keepdims=True)
        return [summed[k * probes_n : (k + 1) * probes_n] for k in range(3)]

    def spread(values):
        return jnp.concatenate(
            [jnp.broadcast_to(values[p : p + 1, :], (blocks, sounds)) for p in range(probes_n)],
            axis=0,
        )

    fetch.wait()
    send_probes.wait_recv()
    probe = jnp.concatenate([pbuf[0], pbuf[1]], axis=1)
    back(probe, 0)

    lax.fori_loop(early_tiles, 2 * tiles, build, 0)

    collect(meta, 0)
    weight_rows = meta[me, 0:blocks, 0:n]
    mixed = jnp.dot(weight_rows, temporal_ref[...], precision=highest, preferred_element_type=F32)
    if span > n:
        mixed = jnp.concatenate([mixed, jnp.zeros((blocks, span - n), F32)], axis=1)
    asks = jnp.concatenate([mixed, jnp.where(lane == span - 1, 1.0, 0.0)], axis=0)
    every = meta[...].reshape(n * win_tiles * blocks, span)
    answer = lax.dot_general(
        asks, every, (((1,), (1,)), ((), ())), precision=highest, preferred_element_type=F32
    )
    gram = answer[0:blocks] * kernel_scale
    place = answer[blocks : 2 * blocks]
    mixer = jnp.concatenate(
        [jnp.where(jnp.abs(place - t) < 0.5, gram, 0.0) for t in range(tiles)], axis=0
    )
    mixer_high = mixer.astype(BF16)
    mixer_pair = (mixer_high, (mixer - mixer_high.astype(F32)).astype(BF16))

    image = forth(mixer_pair, 0)
    back(image, 1)
    start_sums([(probe, probe), (probe, image), (image, image)], 0)
    second = forth(mixer_pair, 1)
    pp, pw, ww = end_sums(0)
    scale = jnp.sqrt(pp / total + epsilon)
    alpha_one = pw / (scale * scale * total)
    rest = (ww - 2.0 * alpha_one * pw + alpha_one * alpha_one * pp) / (scale * scale * total)
    beta_one = jnp.sqrt(jnp.maximum(rest, 0.0) + epsilon)
    shrink = spread(1.0 / (scale * beta_one))
    alpha_wide = spread(alpha_one)
    next_q = (image - alpha_wide * probe) * shrink
    next_w = (second - alpha_wide * image) * shrink - spread(beta_one / scale) * probe
    start_sums([(next_q, next_w), (next_w, next_w), (next_q, next_q)], 1)
    qw, ww, qq = end_sums(1)
    alpha_two = qw / total
    rest = (ww - 2.0 * alpha_two * qw + alpha_two * alpha_two * qq) / total
    beta_two = jnp.sqrt(jnp.maximum(rest, 0.0) + epsilon)
    residual = next_w - spread(alpha_two) * next_q
    own = jnp.where(half == 0, residual[:, 0:half_sounds], residual[:, half_sounds:])
    for p in range(probes_n):
        residual_ref[:, p, :] = own[p * blocks : (p + 1) * blocks]
    shape = (probes_n, probes_n)
    corner = lax.broadcasted_iota(jnp.int32, shape, 0) == lax.broadcasted_iota(jnp.int32, shape, 1)
    for k, column in enumerate([alpha_one, beta_one, alpha_two, beta_two]):
        coef_ref[k : k + 1, :] = jnp.sum(
            jnp.where(corner, jnp.broadcast_to(column, shape), 0.0), axis=0, keepdims=True
        )

    send_probes.wait_send()
    drain(meta, 0)
    for step in range(2):
        drain(terms.at[step], 1 + step)
        drain(stats.at[step], 3 + step)


def body(probes, footprints, lag_weights, owners, window_tiles, coords, temporal):
    n = lax.axis_size("period")
    blocks, probes_n, half_sounds = probes.shape
    sounds, window = footprints.shape[1:]
    half_cells = coords.shape[1] // 2
    tiles = half_cells // LANES
    rows = probes_n * blocks
    span = LANES * -(-(n + 1) // LANES)
    entries = window // LANES * blocks
    wide = 2 * LANES if tiles % 2 == 0 else LANES
    stat_rows = 8 * -(-3 * probes_n // 8)
    vmem = pl.BlockSpec(memory_space=pltpu.VMEM)
    return pl.pallas_call(
        functools.partial(kernel, n),
        out_shape=(
            jax.ShapeDtypeStruct((4, probes_n), F32),
            jax.ShapeDtypeStruct(probes.shape, F32),
        ),
        in_specs=[vmem, pl.BlockSpec(memory_space=pl.ANY)] + [vmem] * 5,
        out_specs=(vmem, vmem),
        scratch_shapes=[
            pltpu.VMEM(footprints.shape, BF16),
            pltpu.VMEM((2, rows, half_sounds), F32),
            pltpu.VMEM((n, entries, span), F32),
            pltpu.VMEM((2, n, entries, probes_n * LANES), BF16),
            pltpu.VMEM((2, n, stat_rows, LANES), F32),
            pltpu.VMEM((2, rows, half_cells), BF16),
            pltpu.VMEM((2, rows, half_cells), BF16),
            pltpu.VMEM((2, rows, sounds), F32),
            pltpu.VMEM((2, rows, sounds), F32),
            pltpu.VMEM((half_cells // wide, 2 * half_cells, wide), BF16),
            pltpu.VMEM((tiles, rows, LANES), F32),
            pltpu.SemaphoreType.DMA,
            pltpu.SemaphoreType.DMA((5,)),
            pltpu.SemaphoreType.DMA((5,)),
            pltpu.SemaphoreType.DMA((5, n)),
            pltpu.SemaphoreType.DMA((5, n)),
        ],
        compiler_params=pltpu.CompilerParams(
            collective_id=0, has_side_effects=True, vmem_limit_bytes=48 * 1024 * 1024
        ),
    )(probes, footprints, lag_weights, owners, window_tiles, coords, temporal)


def solution(mesh):
    in_specs = (
        P("period", None, "half"),
        P("period", None, "half"),
        P("period", None),
        P("period", None),
        P("period", "half"),
        P(),
        P(),
    )
    out_specs = (P(), P("period", None, "half"))
    return jax.shard_map(body, mesh=mesh, in_specs=in_specs, out_specs=out_specs, check_vma=False)
```

```python
import functools
import math

import jax
import jax.numpy as jnp
from jax import lax
from jax.experimental import pallas as pl
from jax.experimental.pallas import tpu as pltpu
from jax.sharding import PartitionSpec as P

epsilon = 1e-06
kernel_scale = 0.05
kernel_length = 6.0
highest = lax.Precision.HIGHEST
MESH = pl.DeviceIdType.MESH
F32 = jnp.float32
BF16 = jnp.bfloat16
LANES = 128
first_tiles = 5
early_tiles = 9


def kernel(
    n,
    probes_hbm,
    foot_hbm,
    lag_hbm,
    owner_hbm,
    tile_hbm,
    coords_hbm,
    temporal_hbm,
    coef_ref,
    residual_ref,
    probes_ref,
    foot,
    lag_ref,
    owner_ref,
    tile_ref,
    coords_ref,
    temporal_ref,
    pbuf,
    meta,
    terms,
    stats,
    flux_out,
    flux_in,
    image_out,
    image_in,
    kbuf,
    zt,
    features,
    fetch_sem,
    pair_send,
    pair_recv,
    peer_send,
    peer_recv,
):
    me = lax.axis_index("period")
    half = lax.axis_index("half")
    blocks, probes_n, half_sounds = probes_ref.shape
    sounds, window = foot.shape[1:]
    win_tiles = window // LANES
    half_cells = coords_ref.shape[1] // 2
    tiles = half_cells // LANES
    rows = probes_n * blocks
    total = float(n * blocks * sounds)

    arguments = [
        (coords_hbm, coords_ref),
        (probes_hbm, probes_ref),
        (lag_hbm, lag_ref),
        (owner_hbm, owner_ref),
        (tile_hbm, tile_ref),
        (temporal_hbm, temporal_ref),
        (foot_hbm, foot),
    ]
    fetches = [
        pltpu.make_async_copy(source, target, fetch_sem.at[k])
        for k, (source, target) in enumerate(arguments)
    ]
    for fetch in fetches:
        fetch.start()

    barrier = pltpu.get_barrier_semaphore()

    def greet(k, carry):
        pl.semaphore_signal(
            barrier, inc=1, device_id={"period": lax.rem(me + k, n)}, device_id_type=MESH
        )
        return carry

    lax.fori_loop(1, n, greet, 0)
    pl.semaphore_signal(barrier, inc=1, device_id={"half": 1 - half}, device_id_type=MESH)

    def pair_copy(source, target, which):
        return pltpu.make_async_remote_copy(
            src_ref=source,
            dst_ref=target,
            send_sem=pair_send.at[which],
            recv_sem=pair_recv.at[which],
            device_id={"half": 1 - half},
            device_id_type=MESH,
        )

    def peer_copy(slots, slot, which, k):
        return pltpu.make_async_remote_copy(
            src_ref=slots.at[slot],
            dst_ref=slots.at[slot],
            send_sem=peer_send.at[which, k],
            recv_sem=peer_recv.at[which, k],
            device_id={"period": lax.rem(me + k, n)},
            device_id_type=MESH,
        )

    def share(slots, which):
        def step(k, carry):
            peer_copy(slots, me, which, k).start()
            return carry

        lax.fori_loop(1, n, step, 0)

    def collect(slots, which):
        def step(k, carry):
            peer_copy(slots, lax.rem(me + n - k, n), which, k).wait_recv()
            return carry

        lax.fori_loop(1, n, step, 0)

    def drain(slots, which):
        def step(k, carry):
            peer_copy(slots, me, which, k).wait_send()
            return carry

        lax.fori_loop(1, n, step, 0)

    fetches[0].wait()
    x, y = coords_ref[0:1, :], coords_ref[1:2, :]
    square = x * x + y * y
    upper = jnp.bitwise_and(square, -64)
    ones = jnp.ones_like(x)
    blank = jnp.zeros((LANES - 6, x.shape[1]), F32)

    def feature_rows(parts):
        return jnp.concatenate([part.astype(F32) for part in parts] + [blank], axis=0)

    features[0] = feature_rows([x * -2, y * -2, upper, square - upper, ones, ones])
    features[1] = feature_rows([x, y, ones, ones, upper, square - upper])
    wide = kbuf.shape[2]
    own_start = pl.multiple_of(half * half_cells, LANES)
    rate = -math.log2(math.e) / kernel_length

    def build(i, carry):
        own = i < tiles
        side = jnp.where(own, half, 1 - half)
        start = side * half_cells + jnp.where(own, i, i - tiles) * LANES
        left = jnp.transpose(features[0, :, pl.ds(pl.multiple_of(start, LANES), LANES)])
        left = left.astype(BF16)
        at = pl.multiple_of(i * LANES, LANES)
        for c in range(kbuf.shape[0]):
            right = features[
                1, :, pl.ds(pl.multiple_of(own_start + c * wide, LANES), wide)
            ].astype(BF16)
            squared = jnp.dot(left, right, preferred_element_type=F32)
            power = squared * rate * lax.rsqrt(jnp.maximum(squared, 0.5))
            kbuf[c, pl.ds(at, LANES), :] = jnp.exp2(power).astype(BF16)
        return carry

    lax.fori_loop(0, first_tiles, build, 0)

    for fetch in fetches[1:6]:
        fetch.wait()
    for p in range(probes_n):
        pbuf[half, p * blocks : (p + 1) * blocks, :] = probes_ref[:, p, :]

    span = meta.shape[2]
    lane = lax.broadcasted_iota(jnp.int32, (blocks, span), 1)
    square_shape = (blocks, blocks)
    diagonal = lax.broadcasted_iota(jnp.int32, square_shape, 0) == lax.broadcasted_iota(
        jnp.int32, square_shape, 1
    )

    def upright(row):
        spread_row = jnp.broadcast_to(row.astype(F32), square_shape)
        return jnp.sum(jnp.where(diagonal, spread_row, 0.0), axis=1, keepdims=True)

    weight = jnp.zeros((blocks, span), F32)
    for k in range(lag_ref.shape[0]):
        chosen = upright(owner_ref[k : k + 1, :]) == lane.astype(F32)
        weight = weight + jnp.where(chosen, upright(lag_ref[k : k + 1, :]), 0.0)
    tile_column = upright(tile_ref[0:1, :])
    meta[me] = jnp.where(lane == span - 1, tile_column, weight)

    pl.semaphore_wait(barrier, n)
    send_probes = pair_copy(pbuf.at[half], pbuf.at[half], 0)
    send_probes.start()
    share(meta, 0)

    lax.fori_loop(first_tiles, early_tiles, build, 0)

    row_block = lax.rem(lax.broadcasted_iota(jnp.int32, (rows, LANES), 0), blocks)

    def own_rows(values, b):
        keep = jnp.concatenate([row_block] * (values.shape[1] // LANES), axis=1) == b
        return jnp.where(keep, values, 0.0)

    def back(vector, step):
        part = jnp.zeros((rows, window), F32)
        for b in range(blocks):
            part = part + jnp.dot(
                own_rows(vector, b).astype(BF16), foot[b], preferred_element_type=F32
            )
        by_tile = [
            jnp.concatenate(
                [
                    part[p * blocks : (p + 1) * blocks, j * LANES : (j + 1) * LANES]
                    for p in range(probes_n)
                ],
                axis=1,
            )
            for j in range(win_tiles)
        ]
        terms[step, me] = jnp.concatenate(by_tile, axis=0).astype(BF16)
        share(terms.at[step], 1 + step)

    tile_rows = jnp.concatenate(
        [jnp.broadcast_to(tile_column, (blocks, LANES))] * probes_n, axis=0
    )

    def forth(mixer, step):
        collect(terms.at[step], 1 + step)
        shared = terms[step].reshape(n * win_tiles * blocks, probes_n * LANES)
        flux = jnp.dot(mixer[0], shared, preferred_element_type=F32) + jnp.dot(
            mixer[1], shared, preferred_element_type=F32
        )
        flux_out[step] = jnp.concatenate(
            [
                jnp.concatenate(
                    [
                        flux[t * blocks : (t + 1) * blocks, p * LANES : (p + 1) * LANES]
                        for t in range(tiles)
                    ],
                    axis=1,
                )
                for p in range(probes_n)
            ],
            axis=0,
        ).astype(BF16)
        swap = pair_copy(flux_out.at[step], flux_in.at[step], 1 + 2 * step)
        swap.start()
        each = wide // LANES

        def own_part(c, carry):
            got = jnp.dot(
                flux_out[step], kbuf[c, 0:half_cells, :], preferred_element_type=F32
            )
            for e in range(each):
                zt[c * each + e] = got[:, e * LANES : (e + 1) * LANES]
            return carry

        def other_part(c, carry):
            got = jnp.dot(
                flux_in[step],
                kbuf[c, half_cells : 2 * half_cells, :],
                preferred_element_type=F32,
            )
            for e in range(each):
                zt[c * each + e] += got[:, e * LANES : (e + 1) * LANES]
            return carry

        lax.fori_loop(0, kbuf.shape[0], own_part, 0)
        swap.wait()
        lax.fori_loop(0, kbuf.shape[0], other_part, 0)
        parts = []
        for j in range(win_tiles):
            picked = jnp.zeros((rows, LANES), F32)
            for t in range(tiles):
                picked = jnp.where(jnp.abs(tile_rows + float(j - t)) < 0.5, zt[t], picked)
            parts.append(picked)
        windows = jnp.concatenate(parts, axis=1)
        image = jnp.zeros((rows, sounds), F32)
        for b in range(blocks):
            image = image + lax.dot_general(
                own_rows(windows, b).astype(BF16),
                foot[b],
                (((1,), (1,)), ((), ())),
                preferred_element_type=F32,
            )
        image_out[step] = image
        swap = pair_copy(image_out.at[step], image_in.at[step], 2 + 2 * step)
        swap.start()
        swap.wait()
        return image + image_in[step]

    def folded(left, right):
        products = left * right
        wide_sum = products[:, 0:LANES]
        for e in range(1, sounds // LANES):
            wide_sum = wide_sum + products[:, e * LANES : (e + 1) * LANES]
        return [
            jnp.sum(wide_sum[p * blocks : (p + 1) * blocks], axis=0, keepdims=True)
            for p in range(probes_n)
        ]

    def start_sums(pairs, step):
        found = []
        for left, right in pairs:
            found += folded(left, right)
        shape = (len(found), LANES)
        place = lax.broadcasted_iota(jnp.int32, shape, 1) == lax.broadcasted_iota(
            jnp.int32, shape, 0
        )
        sums = jnp.sum(jnp.concatenate(found, axis=0), axis=1, keepdims=True)
        stats[step, me] = jnp.sum(jnp.where(place, sums, 0.0), axis=0, keepdims=True)
        share(stats.at[step], 3 + step)

    def end_sums(step):
        collect(stats.at[step], 3 + step)
        summed = jnp.broadcast_to(jnp.sum(stats[step], axis=0), (3 * probes_n, LANES))
        place = lax.broadcasted_iota(jnp.int32, summed.shape, 1) == lax.broadcasted_iota(
            jnp.int32, summed.shape, 0
        )
        found = jnp.sum(jnp.where(place, summed, 0.0), axis=1, keepdims=True)
        return [found[k * probes_n : (k + 1) * probes_n] for k in range(3)]

    def spread(values):
        return jnp.concatenate(
            [jnp.broadcast_to(values[p : p + 1, :], (blocks, sounds)) for p in range(probes_n)],
            axis=0,
        )

    fetches[6].wait()
    send_probes.wait_recv()
    probe = jnp.concatenate([pbuf[0], pbuf[1]], axis=1)
    back(probe, 0)

    lax.fori_loop(early_tiles, 2 * tiles, build, 0)

    collect(meta, 0)
    weight_rows = meta[me, 0:blocks, 0:n]
    mixed = jnp.dot(weight_rows, temporal_ref[...], precision=highest, preferred_element_type=F32)
    if span > n:
        mixed = jnp.concatenate([mixed, jnp.zeros((blocks, span - n), F32)], axis=1)
    asks = jnp.concatenate([mixed, jnp.where(lane == span - 1, 1.0, 0.0)], axis=0)
    last = lax.broadcasted_iota(jnp.int32, (n, blocks, span), 2) == span - 1
    every = jnp.stack(
        [meta[...] + jnp.where(last, float(j), 0.0) for j in range(win_tiles)], axis=1
    ).reshape(n * win_tiles * blocks, span)
    answer = lax.dot_general(
        asks, every, (((1,), (1,)), ((), ())), precision=highest, preferred_element_type=F32
    )
    gram = answer[0:blocks] * kernel_scale
    place = answer[blocks : 2 * blocks]
    mixer = jnp.concatenate(
        [jnp.where(jnp.abs(place - t) < 0.5, gram, 0.0) for t in range(tiles)], axis=0
    )
    mixer_high = mixer.astype(BF16)
    mixer_pair = (mixer_high, (mixer - mixer_high.astype(F32)).astype(BF16))

    image = forth(mixer_pair, 0)
    back(image, 1)
    start_sums([(probe, probe), (probe, image), (image, image)], 0)
    second = forth(mixer_pair, 1)
    pp, pw, ww = end_sums(0)
    scale = jnp.sqrt(pp / total + epsilon)
    alpha_one = pw / (scale * scale * total)
    rest = (ww - 2.0 * alpha_one * pw + alpha_one * alpha_one * pp) / (scale * scale * total)
    beta_one = jnp.sqrt(jnp.maximum(rest, 0.0) + epsilon)
    shrink = spread(1.0 / (scale * beta_one))
    alpha_wide = spread(alpha_one)
    next_q = (image - alpha_wide * probe) * shrink
    next_w = (second - alpha_wide * image) * shrink - spread(beta_one / scale) * probe
    start_sums([(next_q, next_w), (next_w, next_w), (next_q, next_q)], 1)
    qw, ww, qq = end_sums(1)
    alpha_two = qw / total
    rest = (ww - 2.0 * alpha_two * qw + alpha_two * alpha_two * qq) / total
    beta_two = jnp.sqrt(jnp.maximum(rest, 0.0) + epsilon)
    residual = next_w - spread(alpha_two) * next_q
    own = jnp.where(half == 0, residual[:, 0:half_sounds], residual[:, half_sounds:])
    for p in range(probes_n):
        residual_ref[:, p, :] = own[p * blocks : (p + 1) * blocks]
    shape = (probes_n, probes_n)
    corner = lax.broadcasted_iota(jnp.int32, shape, 0) == lax.broadcasted_iota(jnp.int32, shape, 1)
    for k, column in enumerate([alpha_one, beta_one, alpha_two, beta_two]):
        coef_ref[k : k + 1, :] = jnp.sum(
            jnp.where(corner, jnp.broadcast_to(column, shape), 0.0), axis=0, keepdims=True
        )

    send_probes.wait_send()
    drain(meta, 0)
    for step in range(2):
        drain(terms.at[step], 1 + step)
        drain(stats.at[step], 3 + step)


def body(probes, footprints, lag_weights, owners, window_tiles, coords, temporal):
    n = lax.axis_size("period")
    blocks, probes_n, half_sounds = probes.shape
    sounds, window = footprints.shape[1:]
    half_cells = coords.shape[1] // 2
    tiles = half_cells // LANES
    rows = probes_n * blocks
    span = LANES * -(-(n + 1) // LANES)
    entries = window // LANES * blocks
    wide = 2 * LANES if tiles % 2 == 0 else LANES
    arguments = (
        probes,
        footprints,
        lag_weights.T,
        owners.T,
        window_tiles.T,
        coords,
        temporal,
    )
    vmem = pl.BlockSpec(memory_space=pltpu.VMEM)
    return pl.pallas_call(
        functools.partial(kernel, n),
        out_shape=(
            jax.ShapeDtypeStruct((4, probes_n), F32),
            jax.ShapeDtypeStruct(probes.shape, F32),
        ),
        in_specs=[pl.BlockSpec(memory_space=pltpu.HBM)] * len(arguments),
        out_specs=(vmem, vmem),
        scratch_shapes=[
            *[pltpu.VMEM(argument.shape, argument.dtype) for argument in arguments],
            pltpu.VMEM((2, rows, half_sounds), F32),
            pltpu.VMEM((n, blocks, span), F32),
            pltpu.VMEM((2, n, entries, probes_n * LANES), BF16),
            pltpu.VMEM((2, n, 1, LANES), F32),
            pltpu.VMEM((2, rows, half_cells), BF16),
            pltpu.VMEM((2, rows, half_cells), BF16),
            pltpu.VMEM((2, rows, sounds), F32),
            pltpu.VMEM((2, rows, sounds), F32),
            pltpu.VMEM((half_cells // wide, 2 * half_cells, wide), BF16),
            pltpu.VMEM((tiles, rows, LANES), F32),
            pltpu.VMEM((2, LANES, 2 * half_cells), F32),
            pltpu.SemaphoreType.DMA((len(arguments),)),
            pltpu.SemaphoreType.DMA((5,)),
            pltpu.SemaphoreType.DMA((5,)),
            pltpu.SemaphoreType.DMA((5, n)),
            pltpu.SemaphoreType.DMA((5, n)),
        ],
        compiler_params=pltpu.CompilerParams(
            collective_id=0, has_side_effects=True, vmem_limit_bytes=48 * 1024 * 1024
        ),
    )(*arguments)


def solution(mesh):
    in_specs = (
        P("period", None, "half"),
        P("period", None, "half"),
        P("period", None),
        P("period", None),
        P("period", "half"),
        P(),
        P(),
    )
    out_specs = (P(), P("period", None, "half"))
    return jax.shard_map(body, mesh=mesh, in_specs=in_specs, out_specs=out_specs, check_vma=False)
```

```python
import functools
import math

import jax
import jax.numpy as jnp
from jax import lax
from jax.experimental import pallas as pl
from jax.experimental.pallas import tpu as pltpu
from jax.sharding import PartitionSpec as P

epsilon = 1e-06
kernel_scale = 0.05
kernel_length = 6.0
highest = lax.Precision.HIGHEST
MESH = pl.DeviceIdType.MESH
F32 = jnp.float32
BF16 = jnp.bfloat16
LANES = 128
first_tiles = 5
early_tiles = 9


def kernel(
    n,
    probes_hbm,
    foot_hbm,
    lag_hbm,
    owner_hbm,
    tile_hbm,
    coords_hbm,
    temporal_hbm,
    coef_ref,
    residual_ref,
    probes_ref,
    foot,
    lag_ref,
    owner_ref,
    tile_ref,
    coords_ref,
    temporal_ref,
    pbuf,
    meta,
    terms,
    stats,
    flux_out,
    flux_in,
    image_out,
    image_in,
    kbuf,
    features,
    fetch_sem,
    pair_send,
    pair_recv,
    peer_send,
    peer_recv,
):
    me = lax.axis_index("period")
    half = lax.axis_index("half")
    blocks, probes_n, half_sounds = probes_ref.shape
    sounds, window = foot.shape[1:]
    win_tiles = window // LANES
    half_cells = coords_ref.shape[1] // 2
    tiles = half_cells // LANES
    rows = probes_n * blocks
    total = float(n * blocks * sounds)

    arguments = [
        (coords_hbm, coords_ref),
        (probes_hbm, probes_ref),
        (lag_hbm, lag_ref),
        (owner_hbm, owner_ref),
        (tile_hbm, tile_ref),
        (temporal_hbm, temporal_ref),
        (foot_hbm, foot),
    ]
    fetches = [
        pltpu.make_async_copy(source, target, fetch_sem.at[k])
        for k, (source, target) in enumerate(arguments)
    ]
    for fetch in fetches:
        fetch.start()

    barrier = pltpu.get_barrier_semaphore()

    def greet(k, carry):
        pl.semaphore_signal(
            barrier, inc=1, device_id={"period": lax.rem(me + k, n)}, device_id_type=MESH
        )
        return carry

    lax.fori_loop(1, n, greet, 0)
    pl.semaphore_signal(barrier, inc=1, device_id={"half": 1 - half}, device_id_type=MESH)

    def pair_copy(source, target, which):
        return pltpu.make_async_remote_copy(
            src_ref=source,
            dst_ref=target,
            send_sem=pair_send.at[which],
            recv_sem=pair_recv.at[which],
            device_id={"half": 1 - half},
            device_id_type=MESH,
        )

    def peer_copy(slots, slot, which, k):
        return pltpu.make_async_remote_copy(
            src_ref=slots.at[slot],
            dst_ref=slots.at[slot],
            send_sem=peer_send.at[which, k],
            recv_sem=peer_recv.at[which, k],
            device_id={"period": lax.rem(me + k, n)},
            device_id_type=MESH,
        )

    def share(slots, which):
        def step(k, carry):
            peer_copy(slots, me, which, k).start()
            return carry

        lax.fori_loop(1, n, step, 0)

    def collect(slots, which):
        def step(k, carry):
            peer_copy(slots, lax.rem(me + n - k, n), which, k).wait_recv()
            return carry

        lax.fori_loop(1, n, step, 0)

    def drain(slots, which):
        def step(k, carry):
            peer_copy(slots, me, which, k).wait_send()
            return carry

        lax.fori_loop(1, n, step, 0)

    fetches[0].wait()
    x, y = coords_ref[0:1, :], coords_ref[1:2, :]
    square = x * x + y * y
    upper = jnp.bitwise_and(square, -64)
    ones = jnp.ones_like(x)
    blank = jnp.zeros((LANES - 6, x.shape[1]), F32)

    def feature_rows(parts):
        return jnp.concatenate([part.astype(F32) for part in parts] + [blank], axis=0)

    features[0] = feature_rows([x * -2, y * -2, upper, square - upper, ones, ones])
    features[1] = feature_rows([x, y, ones, ones, upper, square - upper])
    wide = kbuf.shape[2]
    own_start = pl.multiple_of(half * half_cells, LANES)
    rate = -math.log2(math.e) / kernel_length

    def build(i, carry):
        own = i < tiles
        side = jnp.where(own, half, 1 - half)
        start = side * half_cells + jnp.where(own, i, i - tiles) * LANES
        left = jnp.transpose(features[0, :, pl.ds(pl.multiple_of(start, LANES), LANES)])
        left = left.astype(BF16)
        at = pl.multiple_of(i * LANES, LANES)
        for c in range(kbuf.shape[0]):
            right = features[
                1, :, pl.ds(pl.multiple_of(own_start + c * wide, LANES), wide)
            ].astype(BF16)
            squared = jnp.dot(left, right, preferred_element_type=F32)
            power = squared * rate * lax.rsqrt(jnp.maximum(squared, 0.5))
            kbuf[c, pl.ds(at, LANES), :] = jnp.exp2(power).astype(BF16)
        return carry

    lax.fori_loop(0, first_tiles, build, 0)

    for fetch in fetches[1:6]:
        fetch.wait()
    for p in range(probes_n):
        pbuf[half, p * blocks : (p + 1) * blocks, :] = probes_ref[:, p, :]

    span = meta.shape[2]
    lane = lax.broadcasted_iota(jnp.int32, (blocks, span), 1)
    square_shape = (blocks, blocks)
    diagonal = lax.broadcasted_iota(jnp.int32, square_shape, 0) == lax.broadcasted_iota(
        jnp.int32, square_shape, 1
    )

    def upright(row):
        spread_row = jnp.broadcast_to(row.astype(F32), square_shape)
        return jnp.sum(jnp.where(diagonal, spread_row, 0.0), axis=1, keepdims=True)

    weight = jnp.zeros((blocks, span), F32)
    for k in range(lag_ref.shape[0]):
        chosen = upright(owner_ref[k : k + 1, :]) == lane.astype(F32)
        weight = weight + jnp.where(chosen, upright(lag_ref[k : k + 1, :]), 0.0)
    tile_column = upright(tile_ref[0:1, :])
    meta[me] = jnp.where(lane == span - 1, tile_column, weight)

    pl.semaphore_wait(barrier, n)
    send_probes = pair_copy(pbuf.at[half], pbuf.at[half], 0)
    send_probes.start()
    share(meta, 0)

    lax.fori_loop(first_tiles, early_tiles, build, 0)

    row_block = lax.rem(lax.broadcasted_iota(jnp.int32, (rows, LANES), 0), blocks)

    def own_rows(values, b):
        keep = jnp.concatenate([row_block] * (values.shape[1] // LANES), axis=1) == b
        return jnp.where(keep, values, 0.0)

    def back(vector, step):
        part = jnp.zeros((rows, window), F32)
        for b in range(blocks):
            part = part + jnp.dot(
                own_rows(vector, b).astype(BF16), foot[b], preferred_element_type=F32
            )
        by_tile = [
            jnp.concatenate(
                [
                    part[p * blocks : (p + 1) * blocks, j * LANES : (j + 1) * LANES]
                    for p in range(probes_n)
                ],
                axis=1,
            )
            for j in range(win_tiles)
        ]
        terms[step, me] = jnp.concatenate(by_tile, axis=0).astype(BF16)
        share(terms.at[step], 1 + step)

    tile_rows = jnp.concatenate(
        [jnp.broadcast_to(tile_column, (blocks, LANES))] * probes_n, axis=0
    )

    def forth(mixer, step):
        collect(terms.at[step], 1 + step)
        shared = terms[step].reshape(n * win_tiles * blocks, probes_n * LANES)
        flux = jnp.dot(mixer[0], shared, preferred_element_type=F32) + jnp.dot(
            mixer[1], shared, preferred_element_type=F32
        )
        flux_out[step] = jnp.concatenate(
            [
                jnp.concatenate(
                    [
                        flux[t * blocks : (t + 1) * blocks, p * LANES : (p + 1) * LANES]
                        for t in range(tiles)
                    ],
                    axis=1,
                )
                for p in range(probes_n)
            ],
            axis=0,
        ).astype(BF16)
        swap = pair_copy(flux_out.at[step], flux_in.at[step], 1 + 2 * step)
        swap.start()
        each = wide // LANES

        columns = kbuf.shape[0]
        spatial = [
            jnp.dot(flux_out[step], kbuf[c, 0:half_cells, :], preferred_element_type=F32)
            for c in range(columns)
        ]
        swap.wait()
        spatial = [
            spatial[c]
            + jnp.dot(
                flux_in[step],
                kbuf[c, half_cells : 2 * half_cells, :],
                preferred_element_type=F32,
            )
            for c in range(columns)
        ]
        zt = [
            spatial[t // each][:, t % each * LANES : (t % each + 1) * LANES]
            for t in range(tiles)
        ]
        parts = []
        for j in range(win_tiles):
            picked = jnp.zeros((rows, LANES), F32)
            for t in range(tiles):
                picked = jnp.where(jnp.abs(tile_rows + float(j - t)) < 0.5, zt[t], picked)
            parts.append(picked)
        windows = jnp.concatenate(parts, axis=1)
        image = jnp.zeros((rows, sounds), F32)
        for b in range(blocks):
            image = image + lax.dot_general(
                own_rows(windows, b).astype(BF16),
                foot[b],
                (((1,), (1,)), ((), ())),
                preferred_element_type=F32,
            )
        image_out[step] = image
        swap = pair_copy(image_out.at[step], image_in.at[step], 2 + 2 * step)
        swap.start()
        swap.wait()
        return image + image_in[step]

    def folded(left, right):
        products = left * right
        wide_sum = products[:, 0:LANES]
        for e in range(1, sounds // LANES):
            wide_sum = wide_sum + products[:, e * LANES : (e + 1) * LANES]
        return [
            jnp.sum(wide_sum[p * blocks : (p + 1) * blocks], axis=0, keepdims=True)
            for p in range(probes_n)
        ]

    def start_sums(pairs, step):
        found = []
        for left, right in pairs:
            found += folded(left, right)
        shape = (len(found), LANES)
        place = lax.broadcasted_iota(jnp.int32, shape, 1) == lax.broadcasted_iota(
            jnp.int32, shape, 0
        )
        sums = jnp.sum(jnp.concatenate(found, axis=0), axis=1, keepdims=True)
        stats[step, me] = jnp.sum(jnp.where(place, sums, 0.0), axis=0, keepdims=True)
        share(stats.at[step], 3 + step)

    def end_sums(step):
        collect(stats.at[step], 3 + step)
        summed = jnp.broadcast_to(jnp.sum(stats[step], axis=0), (3 * probes_n, LANES))
        place = lax.broadcasted_iota(jnp.int32, summed.shape, 1) == lax.broadcasted_iota(
            jnp.int32, summed.shape, 0
        )
        found = jnp.sum(jnp.where(place, summed, 0.0), axis=1, keepdims=True)
        return [found[k * probes_n : (k + 1) * probes_n] for k in range(3)]

    def spread(values):
        return jnp.concatenate(
            [jnp.broadcast_to(values[p : p + 1, :], (blocks, sounds)) for p in range(probes_n)],
            axis=0,
        )

    fetches[6].wait()
    send_probes.wait_recv()
    probe = jnp.concatenate([pbuf[0], pbuf[1]], axis=1)
    back(probe, 0)

    lax.fori_loop(early_tiles, 2 * tiles, build, 0)

    collect(meta, 0)
    weight_rows = meta[me, 0:blocks, 0:n]
    mixed = jnp.dot(weight_rows, temporal_ref[...], precision=highest, preferred_element_type=F32)
    if span > n:
        mixed = jnp.concatenate([mixed, jnp.zeros((blocks, span - n), F32)], axis=1)
    asks = jnp.concatenate([mixed, jnp.where(lane == span - 1, 1.0, 0.0)], axis=0)
    last = lax.broadcasted_iota(jnp.int32, (n, blocks, span), 2) == span - 1
    every = jnp.stack(
        [meta[...] + jnp.where(last, float(j), 0.0) for j in range(win_tiles)], axis=1
    ).reshape(n * win_tiles * blocks, span)
    answer = lax.dot_general(
        asks, every, (((1,), (1,)), ((), ())), precision=highest, preferred_element_type=F32
    )
    gram = answer[0:blocks] * kernel_scale
    place = answer[blocks : 2 * blocks]
    mixer = jnp.concatenate(
        [jnp.where(jnp.abs(place - t) < 0.5, gram, 0.0) for t in range(tiles)], axis=0
    )
    mixer_high = mixer.astype(BF16)
    mixer_pair = (mixer_high, (mixer - mixer_high.astype(F32)).astype(BF16))

    image = forth(mixer_pair, 0)
    back(image, 1)
    start_sums([(probe, probe), (probe, image), (image, image)], 0)
    second = forth(mixer_pair, 1)
    pp, pw, ww = end_sums(0)
    scale = jnp.sqrt(pp / total + epsilon)
    alpha_one = pw / (scale * scale * total)
    rest = (ww - 2.0 * alpha_one * pw + alpha_one * alpha_one * pp) / (scale * scale * total)
    beta_one = jnp.sqrt(jnp.maximum(rest, 0.0) + epsilon)
    shrink = spread(1.0 / (scale * beta_one))
    alpha_wide = spread(alpha_one)
    next_q = (image - alpha_wide * probe) * shrink
    next_w = (second - alpha_wide * image) * shrink - spread(beta_one / scale) * probe
    start_sums([(next_q, next_w), (next_w, next_w), (next_q, next_q)], 1)
    qw, ww, qq = end_sums(1)
    alpha_two = qw / total
    rest = (ww - 2.0 * alpha_two * qw + alpha_two * alpha_two * qq) / total
    beta_two = jnp.sqrt(jnp.maximum(rest, 0.0) + epsilon)
    residual = next_w - spread(alpha_two) * next_q
    own = jnp.where(half == 0, residual[:, 0:half_sounds], residual[:, half_sounds:])
    for p in range(probes_n):
        residual_ref[:, p, :] = own[p * blocks : (p + 1) * blocks]
    shape = (probes_n, probes_n)
    corner = lax.broadcasted_iota(jnp.int32, shape, 0) == lax.broadcasted_iota(jnp.int32, shape, 1)
    for k, column in enumerate([alpha_one, beta_one, alpha_two, beta_two]):
        coef_ref[k : k + 1, :] = jnp.sum(
            jnp.where(corner, jnp.broadcast_to(column, shape), 0.0), axis=0, keepdims=True
        )

    send_probes.wait_send()
    drain(meta, 0)
    for step in range(2):
        drain(terms.at[step], 1 + step)
        drain(stats.at[step], 3 + step)


def body(probes, footprints, lag_weights, owners, window_tiles, coords, temporal):
    n = lax.axis_size("period")
    blocks, probes_n, half_sounds = probes.shape
    sounds, window = footprints.shape[1:]
    half_cells = coords.shape[1] // 2
    tiles = half_cells // LANES
    rows = probes_n * blocks
    span = LANES * -(-(n + 1) // LANES)
    entries = window // LANES * blocks
    wide = 2 * LANES if tiles % 2 == 0 else LANES
    arguments = (
        probes,
        footprints,
        lag_weights.T,
        owners.T,
        window_tiles.T,
        coords,
        temporal,
    )
    vmem = pl.BlockSpec(memory_space=pltpu.VMEM)
    return pl.pallas_call(
        functools.partial(kernel, n),
        out_shape=(
            jax.ShapeDtypeStruct((4, probes_n), F32),
            jax.ShapeDtypeStruct(probes.shape, F32),
        ),
        in_specs=[pl.BlockSpec(memory_space=pltpu.HBM)] * len(arguments),
        out_specs=(vmem, vmem),
        scratch_shapes=[
            *[pltpu.VMEM(argument.shape, argument.dtype) for argument in arguments],
            pltpu.VMEM((2, rows, half_sounds), F32),
            pltpu.VMEM((n, blocks, span), F32),
            pltpu.VMEM((2, n, entries, probes_n * LANES), BF16),
            pltpu.VMEM((2, n, 1, LANES), F32),
            pltpu.VMEM((2, rows, half_cells), BF16),
            pltpu.VMEM((2, rows, half_cells), BF16),
            pltpu.VMEM((2, rows, sounds), F32),
            pltpu.VMEM((2, rows, sounds), F32),
            pltpu.VMEM((half_cells // wide, 2 * half_cells, wide), BF16),
            pltpu.VMEM((2, LANES, 2 * half_cells), F32),
            pltpu.SemaphoreType.DMA((len(arguments),)),
            pltpu.SemaphoreType.DMA((5,)),
            pltpu.SemaphoreType.DMA((5,)),
            pltpu.SemaphoreType.DMA((5, n)),
            pltpu.SemaphoreType.DMA((5, n)),
        ],
        compiler_params=pltpu.CompilerParams(
            collective_id=0, has_side_effects=True, vmem_limit_bytes=60 * 1024 * 1024
        ),
    )(*arguments)


def solution(mesh):
    in_specs = (
        P("period", None, "half"),
        P("period", None, "half"),
        P("period", None),
        P("period", None),
        P("period", "half"),
        P(),
        P(),
    )
    out_specs = (P(), P("period", None, "half"))
    return jax.shard_map(body, mesh=mesh, in_specs=in_specs, out_specs=out_specs, check_vma=False)
```

```python
import functools
import math

import jax
import jax.numpy as jnp
from jax import lax
from jax.experimental import pallas as pl
from jax.experimental.pallas import tpu as pltpu
from jax.sharding import PartitionSpec as P

epsilon = 1e-06
kernel_scale = 0.05
kernel_length = 6.0
highest = lax.Precision.HIGHEST
MESH = pl.DeviceIdType.MESH
F32 = jnp.float32
BF16 = jnp.bfloat16
LANES = 128
early_chunks = 1
depth = 16


def kernel(
    n,
    probes_hbm,
    foot_hbm,
    lag_hbm,
    owner_hbm,
    tile_hbm,
    coords_hbm,
    temporal_hbm,
    coef_ref,
    residual_ref,
    probes_ref,
    foot,
    lag_ref,
    owner_ref,
    tile_ref,
    coords_ref,
    temporal_ref,
    pbuf,
    meta,
    terms,
    stats,
    flux_out,
    flux_in,
    image_out,
    image_in,
    kbuf,
    features_in,
    features_out,
    fetch_sem,
    pair_send,
    pair_recv,
    peer_send,
    peer_recv,
):
    me = lax.axis_index("period")
    half = lax.axis_index("half")
    blocks, probes_n, half_sounds = probes_ref.shape
    sounds, window = foot.shape[1:]
    win_tiles = window // LANES
    half_cells = coords_ref.shape[1] // 2
    tiles = half_cells // LANES
    rows = probes_n * blocks
    total = float(n * blocks * sounds)

    arguments = [
        (coords_hbm, coords_ref),
        (probes_hbm, probes_ref),
        (lag_hbm, lag_ref),
        (owner_hbm, owner_ref),
        (tile_hbm, tile_ref),
        (temporal_hbm, temporal_ref),
        (foot_hbm, foot),
    ]
    fetches = [
        pltpu.make_async_copy(source, target, fetch_sem.at[k])
        for k, (source, target) in enumerate(arguments)
    ]
    for fetch in fetches:
        fetch.start()

    barrier = pltpu.get_barrier_semaphore()

    def greet(k, carry):
        pl.semaphore_signal(
            barrier, inc=1, device_id={"period": lax.rem(me + k, n)}, device_id_type=MESH
        )
        return carry

    lax.fori_loop(1, n, greet, 0)
    pl.semaphore_signal(barrier, inc=1, device_id={"half": 1 - half}, device_id_type=MESH)

    def pair_copy(source, target, which):
        return pltpu.make_async_remote_copy(
            src_ref=source,
            dst_ref=target,
            send_sem=pair_send.at[which],
            recv_sem=pair_recv.at[which],
            device_id={"half": 1 - half},
            device_id_type=MESH,
        )

    def peer_copy(slots, slot, which, k):
        return pltpu.make_async_remote_copy(
            src_ref=slots.at[slot],
            dst_ref=slots.at[slot],
            send_sem=peer_send.at[which, k],
            recv_sem=peer_recv.at[which, k],
            device_id={"period": lax.rem(me + k, n)},
            device_id_type=MESH,
        )

    def share(slots, which):
        def step(k, carry):
            peer_copy(slots, me, which, k).start()
            return carry

        lax.fori_loop(1, n, step, 0)

    def collect(slots, which):
        def step(k, carry):
            peer_copy(slots, lax.rem(me + n - k, n), which, k).wait_recv()
            return carry

        lax.fori_loop(1, n, step, 0)

    def drain(slots, which):
        def step(k, carry):
            peer_copy(slots, me, which, k).wait_send()
            return carry

        lax.fori_loop(1, n, step, 0)

    for fetch in fetches[0:6]:
        fetch.wait()
    for p in range(probes_n):
        pbuf[half, p * blocks : (p + 1) * blocks, :] = probes_ref[:, p, :]

    pl.semaphore_wait(barrier, n)
    send_probes = pair_copy(pbuf.at[half], pbuf.at[half], 0)
    send_probes.start()

    span = meta.shape[2]
    lane = lax.broadcasted_iota(jnp.int32, (blocks, span), 1)
    square_shape = (blocks, blocks)
    diagonal = lax.broadcasted_iota(jnp.int32, square_shape, 0) == lax.broadcasted_iota(
        jnp.int32, square_shape, 1
    )

    def upright(row):
        spread_row = jnp.broadcast_to(row.astype(F32), square_shape)
        return jnp.sum(jnp.where(diagonal, spread_row, 0.0), axis=1, keepdims=True)

    weight = jnp.zeros((blocks, span), F32)
    for k in range(lag_ref.shape[0]):
        chosen = upright(owner_ref[k : k + 1, :]) == lane.astype(F32)
        weight = weight + jnp.where(chosen, upright(lag_ref[k : k + 1, :]), 0.0)
    tile_column = upright(tile_ref[0:1, :])
    meta[me] = jnp.where(lane == span - 1, tile_column, weight)
    share(meta, 0)

    x, y = coords_ref[0:1, :], coords_ref[1:2, :]
    square = x * x + y * y
    upper = jnp.bitwise_and(square, -64)
    ones = jnp.ones_like(x)
    blank = jnp.zeros((depth - 6, x.shape[1]), F32)

    def feature_rows(parts):
        return jnp.concatenate([part.astype(F32) for part in parts] + [blank], axis=0)

    features_in[...] = jnp.transpose(
        feature_rows([x * -2, y * -2, upper, square - upper, ones, ones])
    ).astype(BF16)
    features_out[...] = feature_rows([x, y, ones, ones, upper, square - upper]).astype(BF16)
    wide = kbuf.shape[2]
    own_start = pl.multiple_of(half * half_cells, LANES)
    rate = -math.log2(math.e) / kernel_length
    chunk = max(size for size in (1, 2, 3, 4) if tiles % size == 0)
    half_chunks = tiles // chunk
    height = chunk * LANES

    def build(i, carry):
        own = i < half_chunks
        side = jnp.where(own, half, 1 - half)
        start = side * half_cells + jnp.where(own, i, i - half_chunks) * height
        left = features_in[pl.ds(pl.multiple_of(start, height), height), :]
        at = pl.multiple_of(i * height, height)
        for c in range(kbuf.shape[0]):
            right = features_out[:, pl.ds(pl.multiple_of(own_start + c * wide, LANES), wide)]
            squared = jnp.dot(left, right, preferred_element_type=F32)
            power = squared * rate * lax.rsqrt(jnp.maximum(squared, 0.5))
            kbuf[c, pl.ds(at, height), :] = jnp.exp2(power.astype(BF16))
        return carry

    lax.fori_loop(0, early_chunks, build, 0)

    row_block = lax.rem(lax.broadcasted_iota(jnp.int32, (rows, LANES), 0), blocks)

    def own_rows(values, b):
        keep = jnp.concatenate([row_block] * (values.shape[1] // LANES), axis=1) == b
        return jnp.where(keep, values, 0.0)

    def back(vector, step):
        part = jnp.zeros((rows, window), F32)
        for b in range(blocks):
            part = part + jnp.dot(
                own_rows(vector, b).astype(BF16), foot[b], preferred_element_type=F32
            )
        by_tile = [
            jnp.concatenate(
                [
                    part[p * blocks : (p + 1) * blocks, j * LANES : (j + 1) * LANES]
                    for p in range(probes_n)
                ],
                axis=1,
            )
            for j in range(win_tiles)
        ]
        terms[step, me] = jnp.concatenate(by_tile, axis=0).astype(BF16)
        share(terms.at[step], 1 + step)

    tile_rows = jnp.concatenate(
        [jnp.broadcast_to(tile_column, (blocks, LANES))] * probes_n, axis=0
    )

    def forth(mixer, step):
        collect(terms.at[step], 1 + step)
        shared = terms[step].reshape(n * win_tiles * blocks, probes_n * LANES)
        flux = jnp.dot(mixer[0], shared, preferred_element_type=F32) + jnp.dot(
            mixer[1], shared, preferred_element_type=F32
        )
        flux_out[step] = jnp.concatenate(
            [
                jnp.concatenate(
                    [
                        flux[t * blocks : (t + 1) * blocks, p * LANES : (p + 1) * LANES]
                        for t in range(tiles)
                    ],
                    axis=1,
                )
                for p in range(probes_n)
            ],
            axis=0,
        ).astype(BF16)
        swap = pair_copy(flux_out.at[step], flux_in.at[step], 1 + 2 * step)
        swap.start()
        each = wide // LANES

        columns = kbuf.shape[0]
        spatial = [
            jnp.dot(flux_out[step], kbuf[c, 0:half_cells, :], preferred_element_type=F32)
            for c in range(columns)
        ]
        swap.wait()
        spatial = [
            spatial[c]
            + jnp.dot(
                flux_in[step],
                kbuf[c, half_cells : 2 * half_cells, :],
                preferred_element_type=F32,
            )
            for c in range(columns)
        ]
        zt = [
            spatial[t // each][:, t % each * LANES : (t % each + 1) * LANES]
            for t in range(tiles)
        ]
        parts = []
        for j in range(win_tiles):
            picked = jnp.zeros((rows, LANES), F32)
            for t in range(tiles):
                picked = jnp.where(jnp.abs(tile_rows + float(j - t)) < 0.5, zt[t], picked)
            parts.append(picked)
        windows = jnp.concatenate(parts, axis=1)
        image = jnp.zeros((rows, sounds), F32)
        for b in range(blocks):
            image = image + lax.dot_general(
                own_rows(windows, b).astype(BF16),
                foot[b],
                (((1,), (1,)), ((), ())),
                preferred_element_type=F32,
            )
        image_out[step] = image
        swap = pair_copy(image_out.at[step], image_in.at[step], 2 + 2 * step)
        swap.start()
        swap.wait()
        return image + image_in[step]

    def folded(left, right):
        products = left * right
        wide_sum = products[:, 0:LANES]
        for e in range(1, sounds // LANES):
            wide_sum = wide_sum + products[:, e * LANES : (e + 1) * LANES]
        return [
            jnp.sum(wide_sum[p * blocks : (p + 1) * blocks], axis=0, keepdims=True)
            for p in range(probes_n)
        ]

    def start_sums(pairs, step):
        found = []
        for left, right in pairs:
            found += folded(left, right)
        shape = (len(found), LANES)
        place = lax.broadcasted_iota(jnp.int32, shape, 1) == lax.broadcasted_iota(
            jnp.int32, shape, 0
        )
        sums = jnp.sum(jnp.concatenate(found, axis=0), axis=1, keepdims=True)
        stats[step, me] = jnp.sum(jnp.where(place, sums, 0.0), axis=0, keepdims=True)
        share(stats.at[step], 3 + step)

    def end_sums(step):
        collect(stats.at[step], 3 + step)
        summed = jnp.broadcast_to(jnp.sum(stats[step], axis=0), (3 * probes_n, LANES))
        place = lax.broadcasted_iota(jnp.int32, summed.shape, 1) == lax.broadcasted_iota(
            jnp.int32, summed.shape, 0
        )
        found = jnp.sum(jnp.where(place, summed, 0.0), axis=1, keepdims=True)
        return [found[k * probes_n : (k + 1) * probes_n] for k in range(3)]

    def spread(values):
        return jnp.concatenate(
            [jnp.broadcast_to(values[p : p + 1, :], (blocks, sounds)) for p in range(probes_n)],
            axis=0,
        )

    fetches[6].wait()
    send_probes.wait_recv()
    probe = jnp.concatenate([pbuf[0], pbuf[1]], axis=1)
    back(probe, 0)

    lax.fori_loop(early_chunks, 2 * half_chunks, build, 0)

    collect(meta, 0)
    weight_rows = meta[me, 0:blocks, 0:n]
    mixed = jnp.dot(weight_rows, temporal_ref[...], precision=highest, preferred_element_type=F32)
    if span > n:
        mixed = jnp.concatenate([mixed, jnp.zeros((blocks, span - n), F32)], axis=1)
    asks = jnp.concatenate([mixed, jnp.where(lane == span - 1, 1.0, 0.0)], axis=0)
    last = lax.broadcasted_iota(jnp.int32, (n, blocks, span), 2) == span - 1
    every = jnp.stack(
        [meta[...] + jnp.where(last, float(j), 0.0) for j in range(win_tiles)], axis=1
    ).reshape(n * win_tiles * blocks, span)
    answer = lax.dot_general(
        asks, every, (((1,), (1,)), ((), ())), precision=highest, preferred_element_type=F32
    )
    gram = answer[0:blocks] * kernel_scale
    place = answer[blocks : 2 * blocks]
    mixer = jnp.concatenate(
        [jnp.where(jnp.abs(place - t) < 0.5, gram, 0.0) for t in range(tiles)], axis=0
    )
    mixer_high = mixer.astype(BF16)
    mixer_pair = (mixer_high, (mixer - mixer_high.astype(F32)).astype(BF16))

    image = forth(mixer_pair, 0)
    back(image, 1)
    start_sums([(probe, probe), (probe, image), (image, image)], 0)
    second = forth(mixer_pair, 1)
    pp, pw, ww = end_sums(0)
    scale = jnp.sqrt(pp / total + epsilon)
    alpha_one = pw / (scale * scale * total)
    rest = (ww - 2.0 * alpha_one * pw + alpha_one * alpha_one * pp) / (scale * scale * total)
    beta_one = jnp.sqrt(jnp.maximum(rest, 0.0) + epsilon)
    shrink = spread(1.0 / (scale * beta_one))
    alpha_wide = spread(alpha_one)
    next_q = (image - alpha_wide * probe) * shrink
    next_w = (second - alpha_wide * image) * shrink - spread(beta_one / scale) * probe
    start_sums([(next_q, next_w), (next_w, next_w), (next_q, next_q)], 1)
    qw, ww, qq = end_sums(1)
    alpha_two = qw / total
    rest = (ww - 2.0 * alpha_two * qw + alpha_two * alpha_two * qq) / total
    beta_two = jnp.sqrt(jnp.maximum(rest, 0.0) + epsilon)
    residual = next_w - spread(alpha_two) * next_q
    own = jnp.where(half == 0, residual[:, 0:half_sounds], residual[:, half_sounds:])
    for p in range(probes_n):
        residual_ref[:, p, :] = own[p * blocks : (p + 1) * blocks]
    shape = (probes_n, probes_n)
    corner = lax.broadcasted_iota(jnp.int32, shape, 0) == lax.broadcasted_iota(jnp.int32, shape, 1)
    for k, column in enumerate([alpha_one, beta_one, alpha_two, beta_two]):
        coef_ref[k : k + 1, :] = jnp.sum(
            jnp.where(corner, jnp.broadcast_to(column, shape), 0.0), axis=0, keepdims=True
        )

    send_probes.wait_send()
    drain(meta, 0)
    for step in range(2):
        drain(terms.at[step], 1 + step)
        drain(stats.at[step], 3 + step)


def body(probes, footprints, lag_weights, owners, window_tiles, coords, temporal):
    n = lax.axis_size("period")
    blocks, probes_n, half_sounds = probes.shape
    sounds, window = footprints.shape[1:]
    half_cells = coords.shape[1] // 2
    tiles = half_cells // LANES
    rows = probes_n * blocks
    span = LANES * -(-(n + 1) // LANES)
    entries = window // LANES * blocks
    wide = 2 * LANES if tiles % 2 == 0 else LANES
    arguments = (
        probes,
        footprints,
        lag_weights.T,
        owners.T,
        window_tiles.T,
        coords,
        temporal,
    )
    vmem = pl.BlockSpec(memory_space=pltpu.VMEM)
    hbm = pl.BlockSpec(memory_space=pltpu.HBM)
    return pl.pallas_call(
        functools.partial(kernel, n),
        out_shape=(
            jax.ShapeDtypeStruct((4, probes_n), F32),
            jax.ShapeDtypeStruct(probes.shape, F32),
        ),
        in_specs=[hbm] * len(arguments),
        out_specs=(vmem, vmem),
        scratch_shapes=[
            *[pltpu.VMEM(argument.shape, argument.dtype) for argument in arguments],
            pltpu.VMEM((2, rows, half_sounds), F32),
            pltpu.VMEM((n, blocks, span), F32),
            pltpu.VMEM((2, n, entries, probes_n * LANES), BF16),
            pltpu.VMEM((2, n, 1, LANES), F32),
            pltpu.VMEM((2, rows, half_cells), BF16),
            pltpu.VMEM((2, rows, half_cells), BF16),
            pltpu.VMEM((2, rows, sounds), F32),
            pltpu.VMEM((2, rows, sounds), F32),
            pltpu.VMEM((half_cells // wide, 2 * half_cells, wide), BF16),
            pltpu.VMEM((2 * half_cells, depth), BF16),
            pltpu.VMEM((depth, 2 * half_cells), BF16),
            pltpu.SemaphoreType.DMA((len(arguments),)),
            pltpu.SemaphoreType.DMA((5,)),
            pltpu.SemaphoreType.DMA((5,)),
            pltpu.SemaphoreType.DMA((5, n)),
            pltpu.SemaphoreType.DMA((5, n)),
        ],
        compiler_params=pltpu.CompilerParams(
            collective_id=0, has_side_effects=True, vmem_limit_bytes=60 * 1024 * 1024
        ),
    )(*arguments)


def solution(mesh):
    in_specs = (
        P("period", None, "half"),
        P("period", None, "half"),
        P("period", None),
        P("period", None),
        P("period", "half"),
        P(),
        P(),
    )
    out_specs = (P(), P("period", None, "half"))
    return jax.shard_map(body, mesh=mesh, in_specs=in_specs, out_specs=out_specs, check_vma=False)
```

```python
import functools
import math

import jax
import jax.numpy as jnp
from jax import lax
from jax.experimental import pallas as pl
from jax.experimental.pallas import tpu as pltpu
from jax.sharding import PartitionSpec as P

epsilon = 1e-06
kernel_scale = 0.05
kernel_length = 6.0
highest = lax.Precision.HIGHEST
MESH = pl.DeviceIdType.MESH
F32 = jnp.float32
BF16 = jnp.bfloat16
LANES = 128
early_chunks = 1
depth = 16


def kernel(
    n,
    probes_hbm,
    foot_hbm,
    lag_hbm,
    owner_hbm,
    tile_hbm,
    coords_hbm,
    temporal_hbm,
    coef_ref,
    residual_ref,
    probes_ref,
    foot,
    lag_ref,
    owner_ref,
    tile_ref,
    coords_ref,
    temporal_ref,
    pbuf,
    meta,
    terms,
    stats,
    flux_out,
    flux_in,
    image_out,
    image_in,
    kbuf,
    features_in,
    features_out,
    fetch_sem,
    pair_send,
    pair_recv,
    peer_send,
    peer_recv,
):
    me = lax.axis_index("period")
    half = lax.axis_index("half")
    blocks, probes_n, half_sounds = probes_ref.shape
    sounds, window = foot.shape[1:]
    win_tiles = window // LANES
    half_cells = coords_ref.shape[1] // 2
    tiles = half_cells // LANES
    rows = probes_n * blocks
    total = float(n * blocks * sounds)

    arguments = [
        (coords_hbm, coords_ref),
        (probes_hbm, probes_ref),
        (lag_hbm, lag_ref),
        (owner_hbm, owner_ref),
        (tile_hbm, tile_ref),
        (temporal_hbm, temporal_ref),
        (foot_hbm, foot),
    ]
    fetches = [
        pltpu.make_async_copy(source, target, fetch_sem.at[k])
        for k, (source, target) in enumerate(arguments)
    ]
    for fetch in fetches:
        fetch.start()

    barrier = pltpu.get_barrier_semaphore()

    def greet(k, carry):
        pl.semaphore_signal(
            barrier, inc=1, device_id={"period": lax.rem(me + k, n)}, device_id_type=MESH
        )
        return carry

    lax.fori_loop(1, n, greet, 0)
    pl.semaphore_signal(barrier, inc=1, device_id={"half": 1 - half}, device_id_type=MESH)

    def pair_copy(source, target, which):
        return pltpu.make_async_remote_copy(
            src_ref=source,
            dst_ref=target,
            send_sem=pair_send.at[which],
            recv_sem=pair_recv.at[which],
            device_id={"half": 1 - half},
            device_id_type=MESH,
        )

    def peer_copy(slots, slot, which, k):
        return pltpu.make_async_remote_copy(
            src_ref=slots.at[slot],
            dst_ref=slots.at[slot],
            send_sem=peer_send.at[which, k],
            recv_sem=peer_recv.at[which, k],
            device_id={"period": lax.rem(me + k, n)},
            device_id_type=MESH,
        )

    def share(slots, which):
        def step(k, carry):
            peer_copy(slots, me, which, k).start()
            return carry

        lax.fori_loop(1, n, step, 0, unroll=5 if n % 5 == 1 else 1)

    def collect(slots, which):
        def step(k, carry):
            peer_copy(slots, lax.rem(me + n - k, n), which, k).wait_recv()
            return carry

        lax.fori_loop(1, n, step, 0)

    def drain(slots, which):
        def step(k, carry):
            peer_copy(slots, me, which, k).wait_send()
            return carry

        lax.fori_loop(1, n, step, 0)

    for fetch in fetches[0:6]:
        fetch.wait()
    for p in range(probes_n):
        pbuf[half, p * blocks : (p + 1) * blocks, :] = probes_ref[:, p, :]

    pl.semaphore_wait(barrier, n)
    send_probes = pair_copy(pbuf.at[half], pbuf.at[half], 0)
    send_probes.start()

    span = meta.shape[2]
    lane = lax.broadcasted_iota(jnp.int32, (blocks, span), 1)
    square_shape = (blocks, blocks)
    diagonal = lax.broadcasted_iota(jnp.int32, square_shape, 0) == lax.broadcasted_iota(
        jnp.int32, square_shape, 1
    )

    def upright(row):
        spread_row = jnp.broadcast_to(row.astype(F32), square_shape)
        return jnp.sum(jnp.where(diagonal, spread_row, 0.0), axis=1, keepdims=True)

    weight = jnp.zeros((blocks, span), F32)
    for k in range(lag_ref.shape[0]):
        chosen = upright(owner_ref[k : k + 1, :]) == lane.astype(F32)
        weight = weight + jnp.where(chosen, upright(lag_ref[k : k + 1, :]), 0.0)
    tile_column = upright(tile_ref[0:1, :])
    meta[me] = jnp.where(lane == span - 1, tile_column, weight)
    share(meta, 0)

    x, y = coords_ref[0:1, :], coords_ref[1:2, :]
    square = x * x + y * y
    upper = jnp.bitwise_and(square, -64)
    ones = jnp.ones_like(x)
    blank = jnp.zeros((depth - 6, x.shape[1]), F32)

    def feature_rows(parts):
        return jnp.concatenate([part.astype(F32) for part in parts] + [blank], axis=0)

    features_in[...] = jnp.transpose(
        feature_rows([x * -2, y * -2, upper, square - upper, ones, ones])
    ).astype(BF16)
    features_out[...] = feature_rows([x, y, ones, ones, upper, square - upper]).astype(BF16)
    wide = kbuf.shape[2]
    own_start = pl.multiple_of(half * half_cells, LANES)
    rate = -math.log2(math.e) / kernel_length
    chunk = max(size for size in (1, 2, 3, 4) if tiles % size == 0)
    half_chunks = tiles // chunk
    height = chunk * LANES

    def build(i, carry):
        own = i < half_chunks
        side = jnp.where(own, half, 1 - half)
        start = side * half_cells + jnp.where(own, i, i - half_chunks) * height
        left = features_in[pl.ds(pl.multiple_of(start, height), height), :]
        at = pl.multiple_of(i * height, height)
        for c in range(kbuf.shape[0]):
            right = features_out[:, pl.ds(pl.multiple_of(own_start + c * wide, LANES), wide)]
            squared = jnp.dot(left, right, preferred_element_type=F32)
            power = squared * rate * lax.rsqrt(jnp.maximum(squared, 0.5))
            kbuf[c, pl.ds(at, height), :] = jnp.exp2(power.astype(BF16))
        return carry

    lax.fori_loop(0, early_chunks, build, 0)

    row_block = lax.rem(lax.broadcasted_iota(jnp.int32, (rows, LANES), 0), blocks)

    def own_rows(values, b):
        keep = jnp.concatenate([row_block] * (values.shape[1] // LANES), axis=1) == b
        return jnp.where(keep, values, 0.0)

    def back(vector, step):
        part = jnp.zeros((rows, window), F32)
        for b in range(blocks):
            part = part + jnp.dot(
                own_rows(vector, b).astype(BF16), foot[b], preferred_element_type=F32
            )
        by_tile = [
            jnp.concatenate(
                [
                    part[p * blocks : (p + 1) * blocks, j * LANES : (j + 1) * LANES]
                    for p in range(probes_n)
                ],
                axis=1,
            )
            for j in range(win_tiles)
        ]
        terms[step, me] = jnp.concatenate(by_tile, axis=0).astype(BF16)
        share(terms.at[step], 1 + step)

    tile_rows = jnp.concatenate(
        [jnp.broadcast_to(tile_column, (blocks, LANES))] * probes_n, axis=0
    )

    def forth(mixer, step):
        collect(terms.at[step], 1 + step)
        shared = terms[step].reshape(n * win_tiles * blocks, probes_n * LANES)
        flux = jnp.dot(mixer[0], shared, preferred_element_type=F32) + jnp.dot(
            mixer[1], shared, preferred_element_type=F32
        )
        flux_out[step] = jnp.concatenate(
            [
                jnp.concatenate(
                    [
                        flux[t * blocks : (t + 1) * blocks, p * LANES : (p + 1) * LANES]
                        for t in range(tiles)
                    ],
                    axis=1,
                )
                for p in range(probes_n)
            ],
            axis=0,
        ).astype(BF16)
        swap = pair_copy(flux_out.at[step], flux_in.at[step], 1 + 2 * step)
        swap.start()
        each = wide // LANES

        columns = kbuf.shape[0]
        spatial = [
            jnp.dot(flux_out[step], kbuf[c, 0:half_cells, :], preferred_element_type=F32)
            for c in range(columns)
        ]
        swap.wait()
        spatial = [
            spatial[c]
            + jnp.dot(
                flux_in[step],
                kbuf[c, half_cells : 2 * half_cells, :],
                preferred_element_type=F32,
            )
            for c in range(columns)
        ]
        zt = [
            spatial[t // each][:, t % each * LANES : (t % each + 1) * LANES]
            for t in range(tiles)
        ]
        parts = []
        for j in range(win_tiles):
            picked = jnp.zeros((rows, LANES), F32)
            for t in range(tiles):
                picked = jnp.where(jnp.abs(tile_rows + float(j - t)) < 0.5, zt[t], picked)
            parts.append(picked)
        windows = jnp.concatenate(parts, axis=1)
        image = jnp.zeros((rows, sounds), F32)
        for b in range(blocks):
            image = image + lax.dot_general(
                own_rows(windows, b).astype(BF16),
                foot[b],
                (((1,), (1,)), ((), ())),
                preferred_element_type=F32,
            )
        image_out[step] = image
        swap = pair_copy(image_out.at[step], image_in.at[step], 2 + 2 * step)
        swap.start()
        swap.wait()
        return image + image_in[step]

    def folded(left, right):
        products = left * right
        wide_sum = products[:, 0:LANES]
        for e in range(1, sounds // LANES):
            wide_sum = wide_sum + products[:, e * LANES : (e + 1) * LANES]
        return [
            jnp.sum(wide_sum[p * blocks : (p + 1) * blocks], axis=0, keepdims=True)
            for p in range(probes_n)
        ]

    def start_sums(pairs, step):
        found = []
        for left, right in pairs:
            found += folded(left, right)
        shape = (len(found), LANES)
        place = lax.broadcasted_iota(jnp.int32, shape, 1) == lax.broadcasted_iota(
            jnp.int32, shape, 0
        )
        sums = jnp.sum(jnp.concatenate(found, axis=0), axis=1, keepdims=True)
        stats[step, me] = jnp.sum(jnp.where(place, sums, 0.0), axis=0, keepdims=True)
        share(stats.at[step], 3 + step)

    def end_sums(step):
        collect(stats.at[step], 3 + step)
        summed = jnp.broadcast_to(jnp.sum(stats[step], axis=0), (3 * probes_n, LANES))
        place = lax.broadcasted_iota(jnp.int32, summed.shape, 1) == lax.broadcasted_iota(
            jnp.int32, summed.shape, 0
        )
        found = jnp.sum(jnp.where(place, summed, 0.0), axis=1, keepdims=True)
        return [found[k * probes_n : (k + 1) * probes_n] for k in range(3)]

    def spread(values):
        return jnp.concatenate(
            [jnp.broadcast_to(values[p : p + 1, :], (blocks, sounds)) for p in range(probes_n)],
            axis=0,
        )

    fetches[6].wait()
    send_probes.wait_recv()
    probe = jnp.concatenate([pbuf[0], pbuf[1]], axis=1)
    back(probe, 0)

    lax.fori_loop(early_chunks, 2 * half_chunks, build, 0)

    collect(meta, 0)
    weight_rows = meta[me, 0:blocks, 0:n]
    mixed = jnp.dot(weight_rows, temporal_ref[...], precision=highest, preferred_element_type=F32)
    if span > n:
        mixed = jnp.concatenate([mixed, jnp.zeros((blocks, span - n), F32)], axis=1)
    asks = jnp.concatenate([mixed, jnp.where(lane == span - 1, 1.0, 0.0)], axis=0)
    last = lax.broadcasted_iota(jnp.int32, (n, blocks, span), 2) == span - 1
    every = jnp.stack(
        [meta[...] + jnp.where(last, float(j), 0.0) for j in range(win_tiles)], axis=1
    ).reshape(n * win_tiles * blocks, span)
    answer = lax.dot_general(
        asks, every, (((1,), (1,)), ((), ())), precision=highest, preferred_element_type=F32
    )
    gram = answer[0:blocks] * kernel_scale
    place = answer[blocks : 2 * blocks]
    mixer = jnp.concatenate(
        [jnp.where(jnp.abs(place - t) < 0.5, gram, 0.0) for t in range(tiles)], axis=0
    )
    mixer_high = mixer.astype(BF16)
    mixer_pair = (mixer_high, (mixer - mixer_high.astype(F32)).astype(BF16))

    image = forth(mixer_pair, 0)
    back(image, 1)
    start_sums([(probe, probe), (probe, image), (image, image)], 0)
    second = forth(mixer_pair, 1)
    pp, pw, ww = end_sums(0)
    scale = jnp.sqrt(pp / total + epsilon)
    alpha_one = pw / (scale * scale * total)
    rest = (ww - 2.0 * alpha_one * pw + alpha_one * alpha_one * pp) / (scale * scale * total)
    beta_one = jnp.sqrt(jnp.maximum(rest, 0.0) + epsilon)
    shrink = spread(1.0 / (scale * beta_one))
    alpha_wide = spread(alpha_one)
    next_q = (image - alpha_wide * probe) * shrink
    next_w = (second - alpha_wide * image) * shrink - spread(beta_one / scale) * probe
    start_sums([(next_q, next_w), (next_w, next_w), (next_q, next_q)], 1)
    qw, ww, qq = end_sums(1)
    alpha_two = qw / total
    rest = (ww - 2.0 * alpha_two * qw + alpha_two * alpha_two * qq) / total
    beta_two = jnp.sqrt(jnp.maximum(rest, 0.0) + epsilon)
    residual = next_w - spread(alpha_two) * next_q
    own = jnp.where(half == 0, residual[:, 0:half_sounds], residual[:, half_sounds:])
    for p in range(probes_n):
        residual_ref[:, p, :] = own[p * blocks : (p + 1) * blocks]
    shape = (probes_n, probes_n)
    corner = lax.broadcasted_iota(jnp.int32, shape, 0) == lax.broadcasted_iota(jnp.int32, shape, 1)
    for k, column in enumerate([alpha_one, beta_one, alpha_two, beta_two]):
        coef_ref[k : k + 1, :] = jnp.sum(
            jnp.where(corner, jnp.broadcast_to(column, shape), 0.0), axis=0, keepdims=True
        )

    send_probes.wait_send()
    drain(meta, 0)
    for step in range(2):
        drain(terms.at[step], 1 + step)
        drain(stats.at[step], 3 + step)


def body(probes, footprints, lag_weights, owners, window_tiles, coords, temporal):
    n = lax.axis_size("period")
    blocks, probes_n, half_sounds = probes.shape
    sounds, window = footprints.shape[1:]
    half_cells = coords.shape[1] // 2
    tiles = half_cells // LANES
    rows = probes_n * blocks
    span = LANES * -(-(n + 1) // LANES)
    entries = window // LANES * blocks
    wide = 2 * LANES if tiles % 2 == 0 else LANES
    arguments = (
        probes,
        footprints,
        lag_weights.T,
        owners.T,
        window_tiles.T,
        coords,
        temporal,
    )
    vmem = pl.BlockSpec(memory_space=pltpu.VMEM)
    hbm = pl.BlockSpec(memory_space=pltpu.HBM)
    return pl.pallas_call(
        functools.partial(kernel, n),
        out_shape=(
            jax.ShapeDtypeStruct((4, probes_n), F32),
            jax.ShapeDtypeStruct(probes.shape, F32),
        ),
        in_specs=[hbm] * len(arguments),
        out_specs=(vmem, vmem),
        scratch_shapes=[
            *[pltpu.VMEM(argument.shape, argument.dtype) for argument in arguments],
            pltpu.VMEM((2, rows, half_sounds), F32),
            pltpu.VMEM((n, blocks, span), F32),
            pltpu.VMEM((2, n, entries, probes_n * LANES), BF16),
            pltpu.VMEM((2, n, 1, LANES), F32),
            pltpu.VMEM((2, rows, half_cells), BF16),
            pltpu.VMEM((2, rows, half_cells), BF16),
            pltpu.VMEM((2, rows, sounds), F32),
            pltpu.VMEM((2, rows, sounds), F32),
            pltpu.VMEM((half_cells // wide, 2 * half_cells, wide), BF16),
            pltpu.VMEM((2 * half_cells, depth), BF16),
            pltpu.VMEM((depth, 2 * half_cells), BF16),
            pltpu.SemaphoreType.DMA((len(arguments),)),
            pltpu.SemaphoreType.DMA((5,)),
            pltpu.SemaphoreType.DMA((5,)),
            pltpu.SemaphoreType.DMA((5, n)),
            pltpu.SemaphoreType.DMA((5, n)),
        ],
        compiler_params=pltpu.CompilerParams(
            collective_id=0, has_side_effects=True, vmem_limit_bytes=60 * 1024 * 1024
        ),
    )(*arguments)


def solution(mesh):
    in_specs = (
        P("period", None, "half"),
        P("period", None, "half"),
        P("period", None),
        P("period", None),
        P("period", "half"),
        P(),
        P(),
    )
    out_specs = (P(), P("period", None, "half"))
    return jax.shard_map(body, mesh=mesh, in_specs=in_specs, out_specs=out_specs, check_vma=False)
```
